128 devices in a mesh: island: 16 (over z_lo, x, core), fsdp: 8 (over z_hi, y).
Axes of the slice: x: 4, y: 4, z: 4 (z_hi: 2, z_lo: 2; z = z_hi * 2 + z_lo), core: 2. Of those that a mesh axis runs over, the one named last changes fastest.
Arguments:
- acts: bfloat16 [16, 2048, 8192], P('island', 'fsdp'), may hold values from -6 to 6
- cotangent: bfloat16 [16, 2048, 1024], P('island', 'fsdp'), may hold values from -0.125 to 0.125
- inner_weight: float32 [16, 8192, 1024], P('island', 'fsdp'), may hold values from -3 to 3
- first_moment: float32 [16, 8192, 1024], P('island', 'fsdp'), may hold values from -0.6 to 0.6
- second_moment: float32 [16, 8192, 1024], P('island', 'fsdp'), may hold values from 0.02 to 0.2
- outer_weight: float32 [8, 1024, 1024], P('fsdp', 'island'), may hold values from -3 to 3
- outer_momentum: float32 [8, 1024, 1024], P('fsdp', 'island'), may hold values from -1.5 to 1.5
Outputs:
- input_grad: bfloat16 [16, 2048, 8192], P('island', 'fsdp')
- mixed_weight: float32 [16, 8192, 1024], P('island', 'fsdp')
- new_outer: float32 [8, 1024, 1024], P('fsdp', 'island')
- new_momentum: float32 [8, 1024, 1024], P('fsdp', 'island')
The draws below stay inside these ranges and needn't reach their ends.
All inputs are finite; a program needn't handle non-finite values.
Results may differ from the reference program's by a relative error of at most 0.015.
Values may be sent and summed in bfloat16 or wider, within the bound.
No kernel may reach another device: no remote copies, remote signals or barrier semaphores. Data moves between devices by JAX's collectives and lax.ppermute only.
A program may use at most 192 MiB of HBM per device.

```python
import math
import jax
import jax.numpy as jnp
from jax import lax

D = 8192
KV = 1024
TOK_DEV = 256
STEP = 10
TOK_ISL = 2048
N_ISLAND = 16
N_FSDP = 8


def shard_levels(key, dims, pieces, smallest, top_value):
    level, own = 1.0, jax.random.fold_in(key, 6)
    for position, shards_of in pieces:
        steps = jnp.exp(jax.random.uniform(jax.random.fold_in(own, position), (shards_of,), jnp.float32, smallest / len(pieces), top_value / len(pieces)))
        level = level * jnp.repeat(steps, dims[position] // shards_of).reshape([-1 if axis == position else 1 for axis in range(len(dims))])
    return level


def noise(own_key, extent, width, bound, split=(), dtype=jnp.bfloat16):
    drawn = jax.random.normal(own_key, extent, jnp.float32) * width
    if len(split) > 0:
        drawn = shard_levels(own_key, extent, split, -0.22, 0.18) * drawn
    return jnp.clip(drawn, min=-bound, max=bound).astype(dtype)


def setup_inputs(seed: int = 0) -> dict:
    arg_keys = jax.random.split(jax.random.key(seed), 8)
    acts = noise(arg_keys[0], (N_ISLAND, TOK_ISL, D), 1.0, 6.0, ((0, 16), (1, 8)))
    cotangent = noise(arg_keys[1], (N_ISLAND, TOK_ISL, KV), TOK_ISL ** -0.5, 0.125, ((0, 16), (1, 8)))
    inner_weight = noise(arg_keys[2], (N_ISLAND, D, KV), 0.5, 3.0, ((0, 16), (1, 8)), jnp.float32)
    first_moment = noise(arg_keys[3], (N_ISLAND, D, KV), 0.1, 0.6, ((0, 16), (1, 8)), jnp.float32)
    second_moment = jnp.clip(jnp.exp(math.log(0.2) - 2.3025851 * jax.random.uniform(arg_keys[4], (N_ISLAND, D, KV), jnp.float32) ** shard_levels(arg_keys[4], (N_ISLAND, D, KV), ((0, 16), (1, 8)), -0.2, 0.2)), 0.02, 0.2)
    outer_weight = noise(arg_keys[5], (N_FSDP, D // N_FSDP, KV), 0.5, 3.0, ((0, 8), (1, 16)), jnp.float32)
    outer_momentum = noise(arg_keys[6], (N_FSDP, D // N_FSDP, KV), 0.25, 1.5, ((0, 8), (1, 16)), jnp.float32)
    return {"acts": acts, "cotangent": cotangent, "inner_weight": inner_weight, "first_moment": first_moment, "second_moment": second_moment, "outer_weight": outer_weight, "outer_momentum": outer_momentum}


def island_step(operands):
    acts_isl, cot_isl, weight, moment_a, moment_b = operands
    weight_bf = weight.astype(jnp.bfloat16)
    input_grad = jnp.dot(cot_isl, weight_bf.T, preferred_element_type=jnp.float32).astype(jnp.bfloat16)
    acts_groups = acts_isl.reshape(N_FSDP, TOK_DEV, D)
    cot_groups = cot_isl.reshape(N_FSDP, TOK_DEV, KV)

    def add_group(index, total):
        partial_value = jnp.dot(acts_groups[index].T, cot_groups[index], preferred_element_type=jnp.float32)
        partial_value = lax.optimization_barrier(partial_value.astype(jnp.bfloat16))
        return total + partial_value.astype(jnp.float32)
    gradient = lax.fori_loop(0, N_FSDP, add_group, jnp.zeros((D, KV), jnp.float32))
    moment_one = 0.9 * moment_a + 0.1 * gradient
    moment_two = 0.95 * moment_b + 0.05 * gradient * gradient
    correct_one = 1.0 - 0.9 ** STEP
    correct_two = 1.0 - 0.95 ** STEP
    updated = weight - 0.5 * (moment_one / correct_one) / (jnp.sqrt(moment_two / correct_two) + 1e-08)
    return (input_grad, updated)

def reference(acts, cotangent, inner_weight, first_moment, second_moment, outer_weight, outer_momentum):
    input_grad, updated = lax.map(island_step, (acts, cotangent, inner_weight, first_moment, second_moment))
    anchor = outer_weight.reshape(D, KV)
    momentum = outer_momentum.reshape(D, KV)
    pseudo = anchor - lax.optimization_barrier(jnp.sum(updated, axis=0)) / N_ISLAND
    new_momentum = 0.9 * momentum + pseudo
    new_outer = anchor - 0.7 * (pseudo + 0.9 * new_momentum)
    mixed_weight = 0.5 * updated + 0.5 * new_outer[None]
    return (input_grad, mixed_weight, new_outer.reshape(N_FSDP, D // N_FSDP, KV), new_momentum.reshape(N_FSDP, D // N_FSDP, KV))
```

```python
import jax
import jax.numpy as jnp
from jax import lax
from jax.experimental import pallas as pl
from jax.experimental.pallas import tpu as pltpu
from jax.sharding import PartitionSpec as P

STEP = 10
BF = jnp.bfloat16
F32 = jnp.float32
ROWS = 1024
KV = 1024
TOK = 256
MIB = 1 << 20


def f_index(zh, y):
    return (zh % 2) * 4 + y % 4


def along_y(array, step):
    pairs = [(f_index(z, y), f_index(z, y + step)) for z in range(2) for y in range(4)]
    return lax.ppermute(array, "fsdp", pairs)


def swap_z(array):
    pairs = [(f_index(z, y), f_index(z + 1, y)) for z in range(2) for y in range(4)]
    return lax.ppermute(array, "fsdp", pairs)


def island_shift(array, dz, dx, dc):
    def index(z, x, c):
        return ((z % 2) * 4 + x % 4) * 2 + c % 2

    pairs = [
        (index(z, x, c), index(z + dz, x + dx, c + dc))
        for z in range(2)
        for x in range(4)
        for c in range(2)
    ]
    return lax.ppermute(array, "island", pairs)


def cost(flops, moved):
    return pl.CostEstimate(flops=flops, bytes_accessed=moved, transcendentals=0)


def params(mib):
    return pltpu.CompilerParams(vmem_limit_bytes=mib * MIB)


ANY = pl.BlockSpec(memory_space=pl.ANY)


def pack(acts, place):
    def kernel(place_ref, acts_ref, *refs):
        outs, sems = refs[:6], refs[6]
        zh, y = place_ref[0], place_ref[1]
        copies = []
        for n in range(6):
            dz, dy = 1 - n // 3, n % 3 + 1
            block = lax.rem(zh + dz, 2) * 4 + lax.rem(y + dy, 4)
            columns = pl.ds(pl.multiple_of(block * ROWS, ROWS), ROWS)
            copies.append(pltpu.make_async_copy(acts_ref.at[:, columns], outs[n], sems.at[n]))
        for copy in copies:
            copy.start()
        for copy in copies:
            copy.wait()

    outs = pl.pallas_call(
        kernel,
        out_shape=[jax.ShapeDtypeStruct((TOK, ROWS), BF)] * 6,
        in_specs=[pl.BlockSpec(memory_space=pltpu.SMEM), ANY],
        out_specs=[ANY] * 6,
        scratch_shapes=[pltpu.SemaphoreType.DMA((6,))],
        cost_estimate=cost(0, 6 * MIB),
        compiler_params=params(1),
        name="pack_acts",
    )(place, acts)
    return outs[:3], outs[3:]


def t_dot(a, c):
    return lax.dot_general(a, c, (((0,), (0,)), ((), ())), preferred_element_type=F32)


def partial_sums(block, acts, others, cots):
    tile = 256

    def kernel(block_ref, a0, a1, a2, a3, c0, c1, c2, c3, out):
        total = t_dot(a0[...], c0[...])
        for a, c in ((a1, c1), (a2, c2), (a3, c3)):
            total += t_dot(a[...], c[...])
        out[...] = total.astype(BF)

    strip = pl.BlockSpec((TOK, tile), lambda j, s: (0, j))
    whole = pl.BlockSpec((TOK, KV), lambda j, s: (0, 0))
    return pl.pallas_call(
        kernel,
        out_shape=jax.ShapeDtypeStruct((ROWS, KV), BF),
        grid_spec=pltpu.PrefetchScalarGridSpec(
            num_scalar_prefetch=1,
            grid=(ROWS // tile,),
            in_specs=[pl.BlockSpec((TOK, tile), lambda j, s: (0, s[0] * (ROWS // tile) + j))]
            + [strip] * 3
            + [whole] * 4,
            out_specs=pl.BlockSpec((tile, KV), lambda j, s: (j, 0)),
        ),
        cost_estimate=cost(2 * ROWS * KV * 4 * TOK, 6 * MIB),
        compiler_params=params(16),
        name="partial_sums",
    )(block, acts, *others, *cots)


def adam(info, acts, others, cots, received, master, first, second):
    tile = 256
    correct_one = 1.0 - 0.9**STEP
    correct_two = 1.0 - 0.95**STEP

    def kernel(info_ref, a0, a1, a2, a3, c0, c1, c2, c3, got, w, m1, m2, upd, keep, send):
        grad = t_dot(a0[...], c0[...])
        for a, c in ((a1, c1), (a2, c2), (a3, c3)):
            grad += t_dot(a[...], c[...])
        grad += got[...].astype(F32)
        one = 0.9 * m1[...] + 0.1 * grad
        two = 0.95 * m2[...] + 0.05 * grad * grad
        upd[...] = w[...] - 0.5 * (one / correct_one) / (jnp.sqrt(two / correct_two) + 1e-8)
        core = info_ref[1]
        for p in range(tile // 128):
            mine = pl.ds(pl.multiple_of(p * 128 + core * 64, 64), 64)
            other = pl.ds(pl.multiple_of(p * 128 + (1 - core) * 64, 64), 64)
            keep[p] = upd[mine, :].astype(BF)
            send[p] = upd[other, :].astype(BF)

    strip = pl.BlockSpec((TOK, tile), lambda j, s: (0, j))
    whole = pl.BlockSpec((TOK, KV), lambda j, s: (0, 0))
    rows = pl.BlockSpec((tile, KV), lambda j, s: (j, 0))
    halves = pl.BlockSpec((tile // 128, 64, KV), lambda j, s: (j, 0, 0))
    return pl.pallas_call(
        kernel,
        out_shape=[
            jax.ShapeDtypeStruct((ROWS, KV), F32),
            jax.ShapeDtypeStruct((8, 64, KV), BF),
            jax.ShapeDtypeStruct((8, 64, KV), BF),
        ],
        grid_spec=pltpu.PrefetchScalarGridSpec(
            num_scalar_prefetch=1,
            grid=(ROWS // tile,),
            in_specs=[pl.BlockSpec((TOK, tile), lambda j, s: (0, s[0] * (ROWS // tile) + j))]
            + [strip] * 3
            + [whole] * 4
            + [rows] * 4,
            out_specs=[rows, halves, halves],
        ),
        cost_estimate=cost(2 * ROWS * KV * 4 * TOK, 24 * MIB),
        compiler_params=params(32),
        name="adam_step",
    )(info, acts, *others, *cots, received, master, first, second)


def input_blocks(weight, cots):
    def kernel(w, c0, c1, c2, c3, *outs):
        for c, out in zip((c0, c1, c2, c3), outs):
            out[...] = lax.dot_general(
                c[...], w[...], (((1,), (1,)), ((), ())), preferred_element_type=F32
            ).astype(BF)

    tile = 256
    whole = pl.BlockSpec((TOK, KV), lambda j: (0, 0))
    return pl.pallas_call(
        kernel,
        out_shape=[jax.ShapeDtypeStruct((TOK, ROWS), BF)] * 4,
        grid=(ROWS // tile,),
        in_specs=[pl.BlockSpec((tile, KV), lambda j: (j, 0))] + [whole] * 4,
        out_specs=[pl.BlockSpec((TOK, tile), lambda j: (0, j))] * 4,
        cost_estimate=cost(2 * ROWS * KV * 4 * TOK, 6 * MIB),
        compiler_params=params(16),
        name="input_blocks",
    )(weight, *cots)


def assemble(place, blocks, base, dz):
    def kernel(place_ref, *refs):
        ins, out, sems = refs[:4], refs[-2], refs[-1]
        zh, y = place_ref[0], place_ref[1]
        copies = []
        for k in range(4):
            block = lax.rem(zh + dz, 2) * 4 + lax.rem(y + 4 - k, 4)
            columns = pl.ds(pl.multiple_of(block * ROWS, ROWS), ROWS)
            copies.append(pltpu.make_async_copy(ins[k], out.at[:, columns], sems.at[k]))
        for copy in copies:
            copy.start()
        for copy in copies:
            copy.wait()

    extra = [] if base is None else [base]
    return pl.pallas_call(
        kernel,
        out_shape=jax.ShapeDtypeStruct((TOK, 8 * ROWS), BF),
        in_specs=[pl.BlockSpec(memory_space=pltpu.SMEM)] + [ANY] * (4 + len(extra)),
        out_specs=ANY,
        scratch_shapes=[pltpu.SemaphoreType.DMA((4,))],
        input_output_aliases={5: 0} if extra else {},
        cost_estimate=cost(0, 4 * MIB),
        compiler_params=params(1),
        name="assemble",
    )(place, *blocks, *extra)


VM = pl.BlockSpec(memory_space=pltpu.VMEM)
SM = pl.BlockSpec(memory_space=pltpu.SMEM)


def core_sums(x_place, keep, received):
    def kernel(x_ref, keep_ref, got_ref, *outs):
        for dx in range(4):
            target = lax.rem(x_ref[0] + dx, 4)
            for z in range(2):
                total = keep_ref[z * 4 + target].astype(F32) + got_ref[z * 4 + target].astype(F32)
                outs[dx][z] = total.astype(BF)

    return pl.pallas_call(
        kernel,
        out_shape=[jax.ShapeDtypeStruct((2, 64, KV), BF)] * 4,
        in_specs=[SM, VM, VM],
        out_specs=[VM] * 4,
        cost_estimate=cost(0, 3 * MIB),
        compiler_params=params(16),
        name="core_sums",
    )(x_place, keep, received)


def x_sums(z_place, parts):
    def kernel(z_ref, p0, p1, p2, p3, mine, other):
        def total(z):
            return (p0[z].astype(F32) + p1[z].astype(F32)) + (
                p2[z].astype(F32) + p3[z].astype(F32)
            )

        mine[...] = total(z_ref[0])
        other[...] = total(1 - z_ref[0]).astype(BF)

    return pl.pallas_call(
        kernel,
        out_shape=[jax.ShapeDtypeStruct((64, KV), F32), jax.ShapeDtypeStruct((64, KV), BF)],
        in_specs=[SM] + [VM] * 4,
        out_specs=[VM] * 2,
        cost_estimate=cost(0, 2 * MIB),
        compiler_params=params(8),
        name="x_sums",
    )(z_place, *parts)


def outer_step(mine, received, anchor, momentum):
    def kernel(s, got, w, m, new_w, new_m, rounded):
        pseudo = w[...] - (s[...] + got[...].astype(F32)) / 16.0
        speed = 0.9 * m[...] + pseudo
        fresh = w[...] - 0.7 * (pseudo + 0.9 * speed)
        new_w[...] = fresh
        new_m[...] = speed
        rounded[...] = fresh.astype(BF)

    return pl.pallas_call(
        kernel,
        out_shape=[
            jax.ShapeDtypeStruct((64, KV), F32),
            jax.ShapeDtypeStruct((64, KV), F32),
            jax.ShapeDtypeStruct((64, KV), BF),
        ],
        in_specs=[VM] * 4,
        out_specs=[VM] * 3,
        cost_estimate=cost(0, 2 * MIB),
        compiler_params=params(8),
        name="outer_step",
    )(mine, received, anchor, momentum)


def mix(place, updated, blocks):
    def kernel(place_ref, upd, *refs):
        ins, out = refs[:-1], refs[-1]
        step = pl.program_id(0)
        zl, core = place_ref[0], place_ref[2]
        dx, dz = step // 2, lax.rem(step, 2)
        for k in range(4):

            @pl.when(dx == k)
            def _():
                for dc in range(2):
                    c = lax.rem(core + dc, 2)
                    rows = pl.ds(pl.multiple_of(c * 64, 64), 64)
                    fresh = ins[2 * k + dc][dz].astype(F32)
                    out[rows, :] = 0.5 * upd[rows, :] + 0.5 * fresh

    def at(step, place):
        zl = lax.rem(place[0] + lax.rem(step, 2), 2)
        return (zl * 4 + lax.rem(place[1] + 4 - step // 2, 4), 0)

    rows = pl.BlockSpec((128, KV), at)
    block = pl.BlockSpec((2, 64, KV), lambda step, place: (0, 0, 0))
    return pl.pallas_call(
        kernel,
        out_shape=jax.ShapeDtypeStruct((ROWS, KV), F32),
        grid_spec=pltpu.PrefetchScalarGridSpec(
            num_scalar_prefetch=1,
            grid=(8,),
            in_specs=[rows] + [block] * 8,
            out_specs=rows,
        ),
        cost_estimate=cost(0, 10 * MIB),
        compiler_params=params(16),
        name="mix",
    )(place, updated, *blocks)


def shards(
    acts, cotangent, inner_weight, first_moment, second_moment, outer_weight, outer_momentum
):
    acts, cot, master = acts[0], cotangent[0], inner_weight[0]
    f, i = lax.axis_index("fsdp"), lax.axis_index("island")
    zh, y = f // 4, f % 4
    zl, x, core = i // 8, (i // 2) % 4, i % 2
    f_place = jnp.stack([zh, y]).astype(jnp.int32)
    i_place = jnp.stack([zl, x, core]).astype(jnp.int32)

    cots = [cot] + [along_y(cot, k) for k in (1, 2, 3)]
    to_other, to_own = pack(acts, f_place)
    acts_other = [along_y(a, k + 1) for k, a in enumerate(to_other)]
    acts_own = [along_y(a, k + 1) for k, a in enumerate(to_own)]
    weight = master.astype(BF)
    weight_other = swap_z(weight)

    other_block = ((1 - zh) * 4 + y).astype(jnp.int32)[None]
    partial = partial_sums(other_block, acts, acts_other, cots)
    partial_got = swap_z(partial)
    info = jnp.stack([f, core]).astype(jnp.int32)
    updated, keep, send = adam(
        info, acts, acts_own, cots, partial_got, master, first_moment[0], second_moment[0]
    )

    mine = input_blocks(weight, cots)
    mine = [mine[0]] + [along_y(mine[4 - k], k) for k in (1, 2, 3)]
    others = input_blocks(weight_other, cots)
    others = [others[0]] + [along_y(others[4 - k], k) for k in (1, 2, 3)]
    input_grad = assemble(f_place, mine, None, 0)
    input_grad = assemble(f_place, others, input_grad, 1)

    sums = core_sums(x[None].astype(jnp.int32), keep, island_shift(send, 0, 0, 1))
    sums = [sums[0]] + [island_shift(sums[k], 0, k, 0) for k in (1, 2, 3)]
    mine_sum, other_sum = x_sums(zl[None].astype(jnp.int32), sums)
    new_outer, new_momentum, rounded = outer_step(
        mine_sum, island_shift(other_sum, 1, 0, 0), outer_weight[0], outer_momentum[0]
    )
    pair = jnp.stack([rounded, island_shift(rounded, 1, 0, 0)])
    lines = [pair] + [island_shift(pair, 0, k, 0) for k in (1, 2, 3)]
    blocks = []
    for line in lines:
        blocks += [line, island_shift(line, 0, 0, 1)]
    mixed = mix(i_place, updated, blocks)
    return (input_grad[None], mixed[None], new_outer[None], new_momentum[None])


def solution(mesh):
    by_island = P("island", "fsdp", None)
    by_rows = P("fsdp", "island", None)
    return jax.shard_map(
        shards,
        mesh=mesh,
        in_specs=(by_island,) * 5 + (by_rows,) * 2,
        out_specs=(by_island, by_island, by_rows, by_rows),
        check_vma=False,
    )
```

```python
import math

import jax
import jax.numpy as jnp
from jax import lax
from jax.experimental import pallas as pl
from jax.experimental.pallas import tpu as pltpu
from jax.sharding import PartitionSpec as P

STEP = 10
BF = jnp.bfloat16
F32 = jnp.float32
ROWS = 1024
HALF = 512
KV = 1024
TOK = 256
TILE = 256
MIB = 1 << 20
ANY = pl.BlockSpec(memory_space=pl.ANY)
VM = pl.BlockSpec(memory_space=pltpu.VMEM)
SM = pl.BlockSpec(memory_space=pltpu.SMEM)
HBM = pl.BlockSpec(memory_space=pltpu.HBM)
DIMS_T = (((0,), (0,)), ((), ()))
DIMS_N = (((1,), (1,)), ((), ()))


def f_index(zh, y):
    return (zh % 2) * 4 + y % 4


def along_y(array, step):
    pairs = [(f_index(z, y), f_index(z, y + step)) for z in range(2) for y in range(4)]
    return lax.ppermute(array, "fsdp", pairs)


def swap_z(array):
    pairs = [(f_index(z, y), f_index(z + 1, y)) for z in range(2) for y in range(4)]
    return lax.ppermute(array, "fsdp", pairs)


def island_shift(array, dz, dx, dc):
    def index(z, x, c):
        return ((z % 2) * 4 + x % 4) * 2 + c % 2

    pairs = [
        (index(z, x, c), index(z + dz, x + dx, c + dc))
        for z in range(2)
        for x in range(4)
        for c in range(2)
    ]
    return lax.ppermute(array, "island", pairs)


def cost(moved):
    return pl.CostEstimate(flops=0, bytes_accessed=moved, transcendentals=0)


def params(mib):
    return pltpu.CompilerParams(vmem_limit_bytes=mib * MIB)


def in_hbm(array):
    return pltpu.with_memory_space_constraint(array, pltpu.HBM)


def shape(*dims, dtype=BF):
    return jax.ShapeDtypeStruct(dims, dtype)


def gate(array, *earlier):
    def kernel(*refs):
        pass

    return pl.pallas_call(
        kernel,
        out_shape=shape(*array.shape, dtype=array.dtype),
        in_specs=[ANY] * (1 + len(earlier)),
        out_specs=ANY,
        input_output_aliases={0: 0},
        cost_estimate=cost(1),
        compiler_params=params(1),
        name="gate",
    )(array, *earlier)


def pack(place, acts, cot, master):
    tiles = ROWS // TILE

    def kernel(place_ref, acts_ref, cot_ref, w_ref, *refs):
        first, second, third, own, weight, wide, sems, w_sems = refs[:3], refs[3:6], refs[6:9], *refs[9:]
        zh, y = place_ref[0], place_ref[1]

        def columns(z, dy, start, width):
            block = z * 4 + lax.rem(y + dy, 4)
            return acts_ref.at[:, pl.ds(pl.multiple_of(block * ROWS + start, HALF), width)]

        loads = [
            pltpu.make_async_copy(w_ref.at[pl.ds(t * TILE, TILE)], wide.at[t], w_sems.at[t])
            for t in range(tiles)
        ]
        moves = []
        for n in range(3):
            moves.append((cot_ref, first[n].at[:, pl.ds(0, KV)]))
            moves.append((columns(1 - zh, n + 1, 0, HALF), first[n].at[:, pl.ds(KV, HALF)]))
            moves.append((columns(1 - zh, n + 1, HALF, HALF), second[n]))
            moves.append((columns(zh, n + 1, 0, ROWS), third[n]))
        moves.append((columns(1 - zh, 0, 0, ROWS), own.at[:, pl.ds(0, ROWS)]))
        moves.append((columns(zh, 0, 0, ROWS), own.at[:, pl.ds(ROWS, ROWS)]))
        copies = [pltpu.make_async_copy(a, b, sems.at[n]) for n, (a, b) in enumerate(moves)]
        for load in loads:
            load.start()
        for copy in copies:
            copy.start()
        for t, load in enumerate(loads):
            load.wait()
            weight[pl.ds(t * TILE, TILE), :] = wide[t].astype(BF)
        for copy in copies:
            copy.wait()

    outs = pl.pallas_call(
        kernel,
        out_shape=[shape(TOK, KV + HALF)] * 3
        + [shape(TOK, HALF)] * 3
        + [shape(TOK, ROWS)] * 3
        + [shape(TOK, 2 * ROWS), shape(ROWS, KV)],
        in_specs=[SM, HBM, HBM, HBM],
        out_specs=[VM] * 11,
        scratch_shapes=[
            pltpu.VMEM((tiles, TILE, KV), F32),
            pltpu.SemaphoreType.DMA((14,)),
            pltpu.SemaphoreType.DMA((tiles,)),
        ],
        cost_estimate=cost(1),
        compiler_params=params(16),
        name="pack",
    )(place, acts, cot, master)
    return outs[:3], outs[3:6], outs[6:9], *outs[9:]


def group_sums(dtype, acts, cots, earlier=()):
    def kernel(*refs):
        a, c, out = refs[:4], refs[4:8], refs[-1]
        total = None
        for k in range(4):
            term = lax.dot_general(a[k][...], c[k][...], DIMS_T, preferred_element_type=F32)
            total = term if total is None else total + term
        out[...] = total.astype(dtype)

    def strip(first):
        return pl.BlockSpec((TOK, TILE), lambda j: (0, first // TILE + j))

    whole = pl.BlockSpec((TOK, KV), lambda j: (0, 0))
    return pl.pallas_call(
        kernel,
        out_shape=shape(HALF, KV, dtype=dtype),
        grid=(HALF // TILE,),
        in_specs=[strip(first) for _, first in acts] + [whole] * 4 + [ANY] * len(earlier),
        out_specs=pl.BlockSpec((TILE, KV), lambda j: (j, 0)),
        cost_estimate=cost(1),
        compiler_params=params(16),
        name="group_sums",
    )(*[a for a, _ in acts], *cots, *earlier)


def adam(half, core, own, received, master, first, second, earlier):
    tile = 64
    count = HALF // tile
    from_one = 0.5 / (1.0 - 0.9**STEP)
    from_two = 1.0 / math.sqrt(1.0 - 0.95**STEP)

    def kernel(core_ref, g_ref, got_ref, w_ref, m1_ref, m2_ref, *refs):
        upd_ref, keep, send, g, got, w, m1, m2, upd, sems, out_sems = refs[-11:]
        pairs = ((g_ref, g, 0), (got_ref, got, 0), (w_ref, w, 1), (m1_ref, m1, 1), (m2_ref, m2, 1))
        loads = []
        for t in range(count):
            loads.append(
                [
                    pltpu.make_async_copy(
                        src.at[pl.ds(t * tile + far * half * HALF, tile)], dst.at[t], sems.at[n, t]
                    )
                    for n, (src, dst, far) in enumerate(pairs)
                ]
            )
        for row in loads:
            for load in row:
                load.start()
        stores = []
        for t, row in enumerate(loads):
            for load in row:
                load.wait()
            grad = g[t] + got[t].astype(F32)
            one = 0.9 * m1[t] + 0.1 * grad
            two = 0.95 * m2[t] + 0.05 * grad * grad
            root = two * lax.rsqrt(two)
            new = w[t] - from_one * one / (root * from_two + 1e-8)
            upd[t] = new

            @pl.when(core_ref[0] == t % 2)
            def _():
                keep[t // 2] = new.astype(BF)

            @pl.when(core_ref[0] != t % 2)
            def _():
                send[t // 2] = new.astype(BF)

            store = pltpu.make_async_copy(
                upd.at[t], upd_ref.at[pl.ds(t * tile, tile)], out_sems.at[t]
            )
            store.start()
            stores.append(store)
        for store in stores:
            store.wait()

    return pl.pallas_call(
        kernel,
        out_shape=[shape(HALF, KV, dtype=F32), shape(4, 64, KV), shape(4, 64, KV)],
        in_specs=[SM, ANY, ANY, HBM, HBM, HBM] + [ANY] * len(earlier),
        out_specs=[ANY, VM, VM],
        scratch_shapes=[
            pltpu.VMEM((count, tile, KV), F32),
            pltpu.VMEM((count, tile, KV), BF),
        ]
        + [pltpu.VMEM((count, tile, KV), F32)] * 4
        + [pltpu.SemaphoreType.DMA((5, count)), pltpu.SemaphoreType.DMA((count,))],
        cost_estimate=cost(1),
        compiler_params=params(20),
        name="adam_step",
    )(core, own, received, master, first, second, *earlier)


def input_blocks(weight, weight_got, cots, earlier):
    count = ROWS // TILE

    def kernel(w0, w1, c0, c1, c2, c3, *refs):
        outs, joined = refs[-5:-1], refs[-1]
        step = pl.program_id(0)

        @pl.when(step == 0)
        def _():
            for k, c in enumerate((c0, c1, c2, c3)):
                joined[pl.ds(k * TOK, TOK), :] = c[...]

        def fill(w):
            product = lax.dot_general(joined[...], w[...], DIMS_N, preferred_element_type=F32)
            for k, out in enumerate(outs):
                out[...] = product[k * TOK : (k + 1) * TOK].astype(BF)

        @pl.when(step < count)
        def _():
            fill(w0)

        @pl.when(step >= count)
        def _():
            fill(w1)

    def tile(start):
        return pl.BlockSpec((TILE, KV), lambda j: (jnp.clip(j - start, 0, count - 1), 0))

    whole = pl.BlockSpec((TOK, KV), lambda j: (0, 0))
    return pl.pallas_call(
        kernel,
        out_shape=[shape(TOK, 2 * ROWS)] * 4,
        grid=(2 * count,),
        in_specs=[tile(0), tile(count)] + [whole] * 4 + [ANY] * len(earlier),
        out_specs=[pl.BlockSpec((TOK, TILE), lambda j: (0, j))] * 4,
        scratch_shapes=[pltpu.VMEM((4 * TOK, KV), BF)],
        cost_estimate=cost(1),
        compiler_params=params(20),
        name="input_blocks",
    )(weight, weight_got, *cots, *earlier)


def assemble(place, blocks, earlier):
    def kernel(place_ref, *refs):
        ins, out, sems = refs[:4], refs[-2], refs[-1]
        zh, y = place_ref[0], place_ref[1]
        copies = []
        for k in range(4):
            for dz in range(2):
                block = lax.rem(zh + dz, 2) * 4 + lax.rem(y + 4 - k, 4)
                columns = pl.ds(pl.multiple_of(block * ROWS, ROWS), ROWS)
                part = ins[k].at[:, pl.ds(dz * ROWS, ROWS)]
                copies.append(
                    pltpu.make_async_copy(part, out.at[:, columns], sems.at[2 * k + dz])
                )
        for copy in copies:
            copy.start()
        for copy in copies:
            copy.wait()

    return pl.pallas_call(
        kernel,
        out_shape=shape(TOK, 8 * ROWS),
        in_specs=[SM] + [VM] * 4 + [ANY] * len(earlier),
        out_specs=ANY,
        scratch_shapes=[pltpu.SemaphoreType.DMA((8,))],
        cost_estimate=cost(1),
        compiler_params=params(8),
        name="assemble",
    )(place, *blocks, *earlier)


def core_sums(x_place, keep, received):
    def kernel(x_ref, keep_ref, got_ref, *outs):
        for dx in range(4):
            at = lax.rem(x_ref[0] + dx, 4)
            outs[dx][...] = (keep_ref[at].astype(F32) + got_ref[at].astype(F32)).astype(BF)

    return pl.pallas_call(
        kernel,
        out_shape=[shape(64, KV)] * 4,
        in_specs=[SM, VM, VM],
        out_specs=[VM] * 4,
        cost_estimate=cost(1),
        compiler_params=params(4),
        name="core_sums",
    )(x_place, keep, received)


def x_sums(half, zl, parts, anchor, momentum):
    def kernel(z_ref, p0, p1, p2, p3, w, m, wide, rounded):
        total = (p0[...].astype(F32) + p1[...].astype(F32)) + (
            p2[...].astype(F32) + p3[...].astype(F32)
        )
        wide[...] = total
        base = (16.0 / 1.33) * (-0.33 * w[...] - 0.567 * m[...])
        owner = jnp.broadcast_to(z_ref[0] == half, total.shape)
        rounded[...] = (total + jnp.where(owner, base, 0.0)).astype(BF)

    return pl.pallas_call(
        kernel,
        out_shape=[shape(64, KV, dtype=F32), shape(64, KV)],
        in_specs=[SM] + [VM] * 6,
        out_specs=[VM] * 2,
        cost_estimate=cost(1),
        compiler_params=params(4),
        name="x_sums",
    )(zl, *parts, anchor, momentum)


def outer_step(half, zl, mine, received, anchor, momentum, former):
    def kernel(z_ref, s, got, w, m, *refs):
        new_w, new_m, rounded = refs[-3:]
        total = s[...] + got[...].astype(F32)
        pseudo = w[...] - total / 16.0
        speed = 0.9 * m[...] + pseudo
        fresh = w[...] - 0.7 * (pseudo + 0.9 * speed)
        owner = jnp.broadcast_to(z_ref[0] == half, fresh.shape)
        rounded[...] = jnp.where(owner, fresh, (1.33 / 16.0) * total).astype(BF)
        if half:
            new_w[...] = jnp.where(owner, fresh, refs[0][...])
            new_m[...] = jnp.where(owner, speed, refs[1][...])
        else:
            new_w[...] = fresh
            new_m[...] = speed

    return pl.pallas_call(
        kernel,
        out_shape=[shape(64, KV, dtype=F32), shape(64, KV, dtype=F32), shape(64, KV)],
        in_specs=[SM] + [VM] * (4 + len(former)),
        out_specs=[VM] * 3,
        cost_estimate=cost(1),
        compiler_params=params(8),
        name="outer_step",
    )(zl, mine, received, anchor, momentum, *former)


def mix(half, place, updated, blocks, base):
    extra = [] if base is None else [base]

    def kernel(place_ref, upd, *refs):
        ins, out = refs[:8], refs[-1]
        dx = pl.program_id(0)
        for k in range(4):

            @pl.when(dx == k)
            def _():
                for dc in range(2):
                    core = lax.rem(place_ref[1] + dc, 2)
                    rows = pl.ds(pl.multiple_of(core * 64, 64), 64)
                    out[rows, :] = 0.5 * upd[rows, :] + 0.5 * ins[2 * k + dc][...].astype(F32)

    def here(dx, place):
        return (lax.rem(place[0] + 4 - dx, 4), 0)

    def there(dx, place):
        return (half * 4 + lax.rem(place[0] + 4 - dx, 4), 0)

    block = pl.BlockSpec((64, KV), lambda dx, place: (0, 0))
    return pl.pallas_call(
        kernel,
        out_shape=shape(ROWS, KV, dtype=F32),
        grid_spec=pltpu.PrefetchScalarGridSpec(
            num_scalar_prefetch=1,
            grid=(4,),
            in_specs=[pl.BlockSpec((128, KV), here)] + [block] * 8 + [ANY] * len(extra),
            out_specs=pl.BlockSpec((128, KV), there),
        ),
        input_output_aliases={10: 0} if extra else {},
        cost_estimate=cost(1),
        compiler_params=params(8),
        name="mix",
    )(place, updated, *blocks, *extra)


def shards(
    acts, cotangent, inner_weight, first_moment, second_moment, outer_weight, outer_momentum
):
    acts, cot, master = in_hbm(acts[0]), cotangent[0], in_hbm(inner_weight[0])
    moments = in_hbm(first_moment[0]), in_hbm(second_moment[0])
    anchor, momentum = outer_weight[0], outer_momentum[0]
    f, i = lax.axis_index("fsdp"), lax.axis_index("island")
    f_place = jnp.stack([f // 4, f % 4]).astype(jnp.int32)
    x_core = jnp.stack([(i // 2) % 4, i % 2]).astype(jnp.int32)
    zl, core = (i // 8).astype(jnp.int32)[None], (i % 2).astype(jnp.int32)[None]

    first, second, third, own, weight = pack(f_place, acts, in_hbm(cot), master)
    first = [along_y(a, k + 1) for k, a in enumerate(first)]
    weight_got = swap_z(weight)
    second = [along_y(gate(a, first[k]), k + 1) for k, a in enumerate(second)]
    third = [along_y(gate(a, second[k]), k + 1) for k, a in enumerate(third)]
    cots = [cot] + first

    partial_0 = group_sums(BF, [(own, 0)] + [(a, KV) for a in first], cots)
    got_0 = swap_z(partial_0)
    partial_1 = group_sums(
        BF, [(own, HALF)] + [(a, 0) for a in second], cots, [weight_got]
    )
    got_1 = swap_z(partial_1)
    blocks = input_blocks(weight, weight_got, cots, [partial_1])
    near = [along_y(gate(blocks[4 - k], *third), k) for k in (1, 3)]

    mine = [(own, ROWS)] + [(a, 0) for a in third]
    grad_0 = group_sums(F32, mine, cots, [blocks[0]])
    updated_0, keep_0, send_0 = adam(
        0, core, grad_0, got_0, master, *moments, []
    )
    grad_1 = group_sums(F32, [(a, c + HALF) for a, c in mine], cots, [send_0])

    def over_x(keep, send):
        sums = core_sums(x_core, keep, island_shift(send, 0, 0, 1))
        return [sums[0]] + [island_shift(sums[k], 0, k, 0) for k in (1, 2, 3)]

    def spread(fresh):
        lines = [fresh] + [island_shift(fresh, 0, k, 0) for k in (1, 2, 3)]
        return [part for line in lines for part in (line, island_shift(line, 0, 0, 1))]

    wide_0, rounded_0 = x_sums(0, zl, over_x(keep_0, send_0), anchor, momentum)
    updated_1, keep_1, send_1 = adam(
        1, core, grad_1, got_1, master, *moments, [rounded_0]
    )
    *former, fresh_0 = outer_step(
        0, zl, wide_0, island_shift(rounded_0, 1, 0, 0), anchor, momentum, []
    )
    sums_1 = over_x(keep_1, send_1)
    wide_1, rounded_1 = x_sums(1, zl, sums_1, anchor, momentum)
    far = along_y(gate(blocks[2], *near, sums_1[0]), 2)
    lines_0 = spread(gate(fresh_0, sums_1[1]))
    *former, fresh_1 = outer_step(
        1, zl, wide_1, island_shift(rounded_1, 1, 0, 0), anchor, momentum, former
    )
    lines_1 = spread(fresh_1)
    mixed = mix(0, x_core, gate(updated_0, rounded_1), lines_0, None)
    mixed = mix(1, x_core, updated_1, lines_1, mixed)
    input_grad = assemble(f_place, [blocks[0], near[0], far, near[1]], [lines_1[2]])
    new_outer, new_momentum = former
    return (input_grad[None], mixed[None], new_outer[None], new_momentum[None])


def solution(mesh):
    by_island = P("island", "fsdp", None)
    by_rows = P("fsdp", "island", None)
    return jax.shard_map(
        shards,
        mesh=mesh,
        in_specs=(by_island,) * 5 + (by_rows,) * 2,
        out_specs=(by_island, by_island, by_rows, by_rows),
        check_vma=False,
    )
```

```python
import math

import jax
import jax.numpy as jnp
from jax import lax
from jax.experimental import pallas as pl
from jax.experimental.pallas import tpu as pltpu
from jax.sharding import PartitionSpec as P

STEP = 10
BF = jnp.bfloat16
F32 = jnp.float32
ROWS = 1024
HALF = 512
KV = 1024
TOK = 256
TILE = 256
MIB = 1 << 20
ANY = pl.BlockSpec(memory_space=pl.ANY)
VM = pl.BlockSpec(memory_space=pltpu.VMEM)
SM = pl.BlockSpec(memory_space=pltpu.SMEM)
HBM = pl.BlockSpec(memory_space=pltpu.HBM)
DIMS_T = (((0,), (0,)), ((), ()))
DIMS_N = (((1,), (1,)), ((), ()))


def f_index(zh, y):
    return (zh % 2) * 4 + y % 4


def along_y(array, step):
    pairs = [(f_index(z, y), f_index(z, y + step)) for z in range(2) for y in range(4)]
    return lax.ppermute(array, "fsdp", pairs)


def swap_z(array):
    pairs = [(f_index(z, y), f_index(z + 1, y)) for z in range(2) for y in range(4)]
    return lax.ppermute(array, "fsdp", pairs)


def island_shift(array, dz, dx, dc):
    def index(z, x, c):
        return ((z % 2) * 4 + x % 4) * 2 + c % 2

    pairs = [
        (index(z, x, c), index(z + dz, x + dx, c + dc))
        for z in range(2)
        for x in range(4)
        for c in range(2)
    ]
    return lax.ppermute(array, "island", pairs)


def cost(moved):
    return pl.CostEstimate(flops=0, bytes_accessed=moved, transcendentals=0)


def params(mib):
    return pltpu.CompilerParams(vmem_limit_bytes=mib * MIB)


def in_hbm(array):
    return pltpu.with_memory_space_constraint(array, pltpu.HBM)


def shape(*dims, dtype=BF):
    return jax.ShapeDtypeStruct(dims, dtype)


def gate(array, *earlier):
    def kernel(*refs):
        pass

    return pl.pallas_call(
        kernel,
        out_shape=shape(*array.shape, dtype=array.dtype),
        in_specs=[ANY] * (1 + len(earlier)),
        out_specs=ANY,
        input_output_aliases={0: 0},
        cost_estimate=cost(1),
        compiler_params=params(1),
        name="gate",
    )(array, *earlier)


def pack(place, acts, cot, master):
    tiles = ROWS // TILE

    def kernel(place_ref, acts_ref, cot_ref, w_ref, *refs):
        first, second, third, own, weight, wide, sems, w_sems = refs[:3], refs[3:6], refs[6:9], *refs[9:]
        zh, y = place_ref[0], place_ref[1]

        def columns(z, dy, start, width):
            block = z * 4 + lax.rem(y + dy, 4)
            return acts_ref.at[:, pl.ds(pl.multiple_of(block * ROWS + start, HALF), width)]

        loads = [
            pltpu.make_async_copy(w_ref.at[pl.ds(t * TILE, TILE)], wide.at[t], w_sems.at[t])
            for t in range(tiles)
        ]
        moves = []
        for n in range(3):
            moves.append((cot_ref, first[n].at[:, pl.ds(0, KV)]))
            moves.append((columns(1 - zh, n + 1, 0, HALF), first[n].at[:, pl.ds(KV, HALF)]))
            moves.append((columns(1 - zh, n + 1, HALF, HALF), second[n]))
            moves.append((columns(zh, n + 1, 0, ROWS), third[n]))
        moves.append((columns(1 - zh, 0, 0, ROWS), own.at[:, pl.ds(0, ROWS)]))
        moves.append((columns(zh, 0, 0, ROWS), own.at[:, pl.ds(ROWS, ROWS)]))
        copies = [pltpu.make_async_copy(a, b, sems.at[n]) for n, (a, b) in enumerate(moves)]
        for load in loads:
            load.start()
        for copy in copies:
            copy.start()
        for t, load in enumerate(loads):
            load.wait()
            weight[pl.ds(t * TILE, TILE), :] = wide[t].astype(BF)
        for copy in copies:
            copy.wait()

    outs = pl.pallas_call(
        kernel,
        out_shape=[shape(TOK, KV + HALF)] * 3
        + [shape(TOK, HALF)] * 3
        + [shape(TOK, ROWS)] * 3
        + [shape(TOK, 2 * ROWS), shape(ROWS, KV)],
        in_specs=[SM, HBM, HBM, HBM],
        out_specs=[VM] * 11,
        scratch_shapes=[
            pltpu.VMEM((tiles, TILE, KV), F32),
            pltpu.SemaphoreType.DMA((14,)),
            pltpu.SemaphoreType.DMA((tiles,)),
        ],
        cost_estimate=cost(1),
        compiler_params=params(16),
        name="pack",
    )(place, acts, cot, master)
    return outs[:3], outs[3:6], outs[6:9], *outs[9:]


def group_sums(dtype, acts, cots, earlier=()):
    def kernel(*refs):
        a, c, out = refs[:4], refs[4:8], refs[-1]
        total = None
        for k in range(4):
            term = lax.dot_general(a[k][...], c[k][...], DIMS_T, preferred_element_type=F32)
            total = term if total is None else total + term
        out[...] = total.astype(dtype)

    def strip(first):
        return pl.BlockSpec((TOK, TILE), lambda j: (0, first // TILE + j))

    whole = pl.BlockSpec((TOK, KV), lambda j: (0, 0))
    return pl.pallas_call(
        kernel,
        out_shape=shape(HALF, KV, dtype=dtype),
        grid=(HALF // TILE,),
        in_specs=[strip(first) for _, first in acts] + [whole] * 4 + [ANY] * len(earlier),
        out_specs=pl.BlockSpec((TILE, KV), lambda j: (j, 0)),
        cost_estimate=cost(1),
        compiler_params=params(16),
        name="group_sums",
    )(*[a for a, _ in acts], *cots, *earlier)


def adam(half, core, own, received, master, first, second, earlier):
    tile = 64
    count = HALF // tile
    from_one = 0.5 / (1.0 - 0.9**STEP)
    from_two = 1.0 / math.sqrt(1.0 - 0.95**STEP)

    def kernel(core_ref, g_ref, got_ref, w_ref, m1_ref, m2_ref, *refs):
        upd_ref, keep, send, g, got, w, m1, m2, upd, sems, out_sems = refs[-11:]
        pairs = ((g_ref, g, 0), (got_ref, got, 0), (w_ref, w, 1), (m1_ref, m1, 1), (m2_ref, m2, 1))
        loads = []
        for t in range(count):
            loads.append(
                [
                    pltpu.make_async_copy(
                        src.at[pl.ds(t * tile + far * half * HALF, tile)], dst.at[t], sems.at[n, t]
                    )
                    for n, (src, dst, far) in enumerate(pairs)
                ]
            )
        for row in loads:
            for load in row:
                load.start()
        stores = []
        for t, row in enumerate(loads):
            for load in row:
                load.wait()
            grad = g[t] + got[t].astype(F32)
            one = 0.9 * m1[t] + 0.1 * grad
            two = 0.95 * m2[t] + 0.05 * grad * grad
            root = two * lax.rsqrt(two)
            new = w[t] - from_one * one / (root * from_two + 1e-8)
            upd[t] = new

            @pl.when(core_ref[0] == t % 2)
            def _():
                keep[t // 2] = new.astype(BF)

            @pl.when(core_ref[0] != t % 2)
            def _():
                send[t // 2] = new.astype(BF)

            store = pltpu.make_async_copy(
                upd.at[t], upd_ref.at[pl.ds(t * tile, tile)], out_sems.at[t]
            )
            store.start()
            stores.append(store)
        for store in stores:
            store.wait()

    return pl.pallas_call(
        kernel,
        out_shape=[shape(HALF, KV, dtype=F32), shape(4, 64, KV), shape(4, 64, KV)],
        in_specs=[SM, ANY, ANY, HBM, HBM, HBM] + [ANY] * len(earlier),
        out_specs=[ANY, VM, VM],
        scratch_shapes=[
            pltpu.VMEM((count, tile, KV), F32),
            pltpu.VMEM((count, tile, KV), BF),
        ]
        + [pltpu.VMEM((count, tile, KV), F32)] * 4
        + [pltpu.SemaphoreType.DMA((5, count)), pltpu.SemaphoreType.DMA((count,))],
        cost_estimate=cost(1),
        compiler_params=params(20),
        name="adam_step",
    )(core, own, received, master, first, second, *earlier)


def input_blocks(weight, weight_got, cots, earlier):
    count = ROWS // TILE

    def kernel(w0, w1, c0, c1, c2, c3, *refs):
        outs, joined = refs[-5:-1], refs[-1]
        step = pl.program_id(0)

        @pl.when(step == 0)
        def _():
            for k, c in enumerate((c0, c1, c2, c3)):
                joined[pl.ds(k * TOK, TOK), :] = c[...]

        def fill(w):
            product = lax.dot_general(joined[...], w[...], DIMS_N, preferred_element_type=F32)
            for k, out in enumerate(outs):
                out[...] = product[k * TOK : (k + 1) * TOK].astype(BF)

        @pl.when(step < count)
        def _():
            fill(w0)

        @pl.when(step >= count)
        def _():
            fill(w1)

    def tile(start):
        return pl.BlockSpec((TILE, KV), lambda j: (jnp.clip(j - start, 0, count - 1), 0))

    whole = pl.BlockSpec((TOK, KV), lambda j: (0, 0))
    return pl.pallas_call(
        kernel,
        out_shape=[pltpu.HBM((TOK, 2 * ROWS), BF)] * 4,
        grid=(2 * count,),
        in_specs=[tile(0), tile(count)] + [whole] * 4 + [ANY] * len(earlier),
        out_specs=[pl.BlockSpec((TOK, TILE), lambda j: (0, j))] * 4,
        scratch_shapes=[pltpu.VMEM((4 * TOK, KV), BF)],
        cost_estimate=cost(1),
        compiler_params=params(20),
        name="input_blocks",
    )(weight, weight_got, *cots, *earlier)


def assemble(place, blocks, earlier):
    def kernel(place_ref, *refs):
        ins, out, sems = refs[:4], refs[-2], refs[-1]
        zh, y = place_ref[0], place_ref[1]
        copies = []
        for k in range(4):
            for dz in range(2):
                block = lax.rem(zh + dz, 2) * 4 + lax.rem(y + 4 - k, 4)
                columns = pl.ds(pl.multiple_of(block * ROWS, ROWS), ROWS)
                part = ins[k].at[:, pl.ds(dz * ROWS, ROWS)]
                copies.append(
                    pltpu.make_async_copy(part, out.at[:, columns], sems.at[2 * k + dz])
                )
        for copy in copies:
            copy.start()
        for copy in copies:
            copy.wait()

    return pl.pallas_call(
        kernel,
        out_shape=shape(TOK, 8 * ROWS),
        in_specs=[SM] + [VM] * 4 + [ANY] * len(earlier),
        out_specs=ANY,
        scratch_shapes=[pltpu.SemaphoreType.DMA((8,))],
        cost_estimate=cost(1),
        compiler_params=params(8),
        name="assemble",
    )(place, *blocks, *earlier)


def core_sums(x_place, keep, received):
    def kernel(x_ref, keep_ref, got_ref, *outs):
        for dx in range(4):
            at = lax.rem(x_ref[0] + dx, 4)
            outs[dx][...] = (keep_ref[at].astype(F32) + got_ref[at].astype(F32)).astype(BF)

    return pl.pallas_call(
        kernel,
        out_shape=[shape(64, KV)] * 4,
        in_specs=[SM, VM, VM],
        out_specs=[VM] * 4,
        cost_estimate=cost(1),
        compiler_params=params(4),
        name="core_sums",
    )(x_place, keep, received)


def x_sums(half, zl, parts, anchor, momentum):
    def kernel(z_ref, p0, p1, p2, p3, w, m, wide, rounded):
        total = (p0[...].astype(F32) + p1[...].astype(F32)) + (
            p2[...].astype(F32) + p3[...].astype(F32)
        )
        wide[...] = total
        base = (16.0 / 1.33) * (-0.33 * w[...] - 0.567 * m[...])
        owner = jnp.broadcast_to(z_ref[0] == half, total.shape)
        rounded[...] = (total + jnp.where(owner, base, 0.0)).astype(BF)

    return pl.pallas_call(
        kernel,
        out_shape=[shape(64, KV, dtype=F32), shape(64, KV)],
        in_specs=[SM] + [VM] * 6,
        out_specs=[VM] * 2,
        cost_estimate=cost(1),
        compiler_params=params(4),
        name="x_sums",
    )(zl, *parts, anchor, momentum)


def outer_step(half, zl, mine, received, anchor, momentum, former):
    def kernel(z_ref, s, got, w, m, *refs):
        new_w, new_m, rounded = refs[-3:]
        total = s[...] + got[...].astype(F32)
        pseudo = w[...] - total / 16.0
        speed = 0.9 * m[...] + pseudo
        fresh = w[...] - 0.7 * (pseudo + 0.9 * speed)
        owner = jnp.broadcast_to(z_ref[0] == half, fresh.shape)
        rounded[...] = jnp.where(owner, fresh, (1.33 / 16.0) * total).astype(BF)
        if half:
            new_w[...] = jnp.where(owner, fresh, refs[0][...])
            new_m[...] = jnp.where(owner, speed, refs[1][...])
        else:
            new_w[...] = fresh
            new_m[...] = speed

    return pl.pallas_call(
        kernel,
        out_shape=[shape(64, KV, dtype=F32), shape(64, KV, dtype=F32), shape(64, KV)],
        in_specs=[SM] + [VM] * (4 + len(former)),
        out_specs=[VM] * 3,
        cost_estimate=cost(1),
        compiler_params=params(8),
        name="outer_step",
    )(zl, mine, received, anchor, momentum, *former)


def mix(half, place, updated, blocks, base):
    extra = [] if base is None else [base]

    def kernel(place_ref, upd, *refs):
        ins, out = refs[:8], refs[-1]
        dx = pl.program_id(0)
        for k in range(4):

            @pl.when(dx == k)
            def _():
                for dc in range(2):
                    core = lax.rem(place_ref[1] + dc, 2)
                    rows = pl.ds(pl.multiple_of(core * 64, 64), 64)
                    out[rows, :] = 0.5 * upd[rows, :] + 0.5 * ins[2 * k + dc][...].astype(F32)

    def here(dx, place):
        return (lax.rem(place[0] + 4 - dx, 4), 0)

    def there(dx, place):
        return (half * 4 + lax.rem(place[0] + 4 - dx, 4), 0)

    block = pl.BlockSpec((64, KV), lambda dx, place: (0, 0))
    return pl.pallas_call(
        kernel,
        out_shape=shape(ROWS, KV, dtype=F32),
        grid_spec=pltpu.PrefetchScalarGridSpec(
            num_scalar_prefetch=1,
            grid=(4,),
            in_specs=[pl.BlockSpec((128, KV), here)] + [block] * 8 + [ANY] * len(extra),
            out_specs=pl.BlockSpec((128, KV), there),
        ),
        input_output_aliases={10: 0} if extra else {},
        cost_estimate=cost(1),
        compiler_params=params(8),
        name="mix",
    )(place, updated, *blocks, *extra)


def shards(
    acts, cotangent, inner_weight, first_moment, second_moment, outer_weight, outer_momentum
):
    acts, cot, master = in_hbm(acts[0]), cotangent[0], in_hbm(inner_weight[0])
    moments = in_hbm(first_moment[0]), in_hbm(second_moment[0])
    anchor, momentum = outer_weight[0], outer_momentum[0]
    f, i = lax.axis_index("fsdp"), lax.axis_index("island")
    f_place = jnp.stack([f // 4, f % 4]).astype(jnp.int32)
    x_core = jnp.stack([(i // 2) % 4, i % 2]).astype(jnp.int32)
    zl, core = (i // 8).astype(jnp.int32)[None], (i % 2).astype(jnp.int32)[None]

    first, second, third, own, weight = pack(f_place, acts, in_hbm(cot), master)
    first = [along_y(a, k + 1) for k, a in enumerate(first)]
    weight_got = swap_z(weight)
    second = [along_y(gate(a, first[k]), k + 1) for k, a in enumerate(second)]
    third = [along_y(gate(a, second[k]), k + 1) for k, a in enumerate(third)]
    cots = [cot] + first

    partial_0 = group_sums(BF, [(own, 0)] + [(a, KV) for a in first], cots)
    got_0 = swap_z(partial_0)
    partial_1 = group_sums(
        BF, [(own, HALF)] + [(a, 0) for a in second], cots, [weight_got]
    )
    got_1 = swap_z(partial_1)
    blocks = [in_hbm(b) for b in input_blocks(weight, weight_got, cots, [partial_1])]
    far = along_y(gate(blocks[2], *third), 2)

    mine = [(own, ROWS)] + [(a, 0) for a in third]
    mine = [(in_hbm(a), c) for a, c in mine]
    cots = [in_hbm(c) for c in cots]
    grad_0 = group_sums(F32, mine, cots, [blocks[0]])
    updated_0, keep_0, send_0 = adam(0, core, grad_0, got_0, master, *moments, [])

    def over_x(keep, send):
        sums = core_sums(x_core, keep, island_shift(send, 0, 0, 1))
        return [sums[0]] + [island_shift(sums[k], 0, k, 0) for k in (1, 2, 3)]

    def with_other_core(lines):
        return [part for line in lines for part in (line, island_shift(line, 0, 0, 1))]

    sums_0 = over_x(keep_0, send_0)
    grad_1 = group_sums(F32, [(a, c + HALF) for a, c in mine], cots)
    wide_0, rounded_0 = x_sums(0, zl, sums_0, anchor, momentum)
    updated_1, keep_1, send_1 = adam(
        1, core, grad_1, got_1, master, *moments, [rounded_0]
    )
    *former, fresh_0 = outer_step(
        0, zl, wide_0, island_shift(rounded_0, 1, 0, 0), anchor, momentum, []
    )
    sums_1 = over_x(keep_1, send_1)
    wide_1, rounded_1 = x_sums(1, zl, sums_1, anchor, momentum)
    near = [along_y(gate(blocks[4 - k], far, rounded_0), k) for k in (1, 3)]
    fresh_0 = gate(fresh_0, sums_1[1])
    lines_0 = with_other_core([fresh_0] + [island_shift(fresh_0, 0, k, 0) for k in (1, 2, 3)])
    *former, fresh_1 = outer_step(
        1, zl, wide_1, island_shift(rounded_1, 1, 0, 0), anchor, momentum, former
    )
    lines_1 = [island_shift(fresh_1, 0, k, 0) for k in (1, 2, 3)]
    mixed = mix(0, x_core, gate(updated_0, rounded_1), lines_0, None)
    input_grad = assemble(f_place, [blocks[0], near[0], far, near[1]], [fresh_1])
    lines_1[1] = gate(lines_1[1], in_hbm(input_grad))
    mixed = mix(1, x_core, updated_1, with_other_core([fresh_1] + lines_1), mixed)
    new_outer, new_momentum = former
    return (input_grad[None], mixed[None], new_outer[None], new_momentum[None])


def solution(mesh):
    by_island = P("island", "fsdp", None)
    by_rows = P("fsdp", "island", None)
    return jax.shard_map(
        shards,
        mesh=mesh,
        in_specs=(by_island,) * 5 + (by_rows,) * 2,
        out_specs=(by_island, by_island, by_rows, by_rows),
        check_vma=False,
    )
```

```python
import math

import jax
import jax.numpy as jnp
from jax import lax
from jax.experimental import pallas as pl
from jax.experimental.pallas import tpu as pltpu
from jax.sharding import PartitionSpec as P

STEP = 10
BF = jnp.bfloat16
F32 = jnp.float32
ROWS = 1024
HALF = 512
KV = 1024
TOK = 256
TILE = 256
MIB = 1 << 20
ANY = pl.BlockSpec(memory_space=pl.ANY)
VM = pl.BlockSpec(memory_space=pltpu.VMEM)
SM = pl.BlockSpec(memory_space=pltpu.SMEM)
HBM = pl.BlockSpec(memory_space=pltpu.HBM)
DIMS_T = (((0,), (0,)), ((), ()))
DIMS_N = (((1,), (1,)), ((), ()))


def f_index(zh, y):
    return (zh % 2) * 4 + y % 4


def along_y(array, step):
    pairs = [(f_index(z, y), f_index(z, y + step)) for z in range(2) for y in range(4)]
    return lax.ppermute(array, "fsdp", pairs)


def swap_z(array):
    pairs = [(f_index(z, y), f_index(z + 1, y)) for z in range(2) for y in range(4)]
    return lax.ppermute(array, "fsdp", pairs)


def island_shift(array, dz, dx, dc):
    def index(z, x, c):
        return ((z % 2) * 4 + x % 4) * 2 + c % 2

    pairs = [
        (index(z, x, c), index(z + dz, x + dx, c + dc))
        for z in range(2)
        for x in range(4)
        for c in range(2)
    ]
    return lax.ppermute(array, "island", pairs)


def cost(moved):
    return pl.CostEstimate(flops=0, bytes_accessed=moved, transcendentals=0)


def params(mib):
    return pltpu.CompilerParams(vmem_limit_bytes=mib * MIB)


def in_hbm(array):
    return pltpu.with_memory_space_constraint(array, pltpu.HBM)


def shape(*dims, dtype=BF):
    return jax.ShapeDtypeStruct(dims, dtype)


def gate(array, *earlier):
    def kernel(*refs):
        pass

    return pl.pallas_call(
        kernel,
        out_shape=shape(*array.shape, dtype=array.dtype),
        in_specs=[ANY] * (1 + len(earlier)),
        out_specs=ANY,
        input_output_aliases={0: 0},
        cost_estimate=cost(1),
        compiler_params=params(1),
        name="gate",
    )(array, *earlier)


def pack(place, acts, cot, master):
    tiles = ROWS // TILE

    def kernel(place_ref, acts_ref, cot_ref, w_ref, *refs):
        first, second, third, own, weight, wide, sems, w_sems = refs[:3], refs[3:6], refs[6:9], *refs[9:]
        zh, y = place_ref[0], place_ref[1]

        def columns(z, dy, start, width):
            block = z * 4 + lax.rem(y + dy, 4)
            return acts_ref.at[:, pl.ds(pl.multiple_of(block * ROWS + start, HALF), width)]

        loads = [
            pltpu.make_async_copy(w_ref.at[pl.ds(t * TILE, TILE)], wide.at[t], w_sems.at[t])
            for t in range(tiles)
        ]
        moves = []
        for n in range(3):
            moves.append((cot_ref, first[n].at[:, pl.ds(0, KV)]))
            moves.append((columns(1 - zh, n + 1, 0, HALF), first[n].at[:, pl.ds(KV, HALF)]))
            moves.append((columns(1 - zh, n + 1, HALF, HALF), second[n]))
            moves.append((columns(zh, n + 1, 0, ROWS), third[n]))
        moves.append((columns(1 - zh, 0, 0, ROWS), own.at[:, pl.ds(0, ROWS)]))
        moves.append((columns(zh, 0, 0, ROWS), own.at[:, pl.ds(ROWS, ROWS)]))
        copies = [pltpu.make_async_copy(a, b, sems.at[n]) for n, (a, b) in enumerate(moves)]
        for load in loads:
            load.start()
        for copy in copies:
            copy.start()
        for t, load in enumerate(loads):
            load.wait()
            weight[pl.ds(t * TILE, TILE), :] = wide[t].astype(BF)
        for copy in copies:
            copy.wait()

    outs = pl.pallas_call(
        kernel,
        out_shape=[shape(TOK, KV + HALF)] * 3
        + [shape(TOK, HALF)] * 3
        + [shape(TOK, ROWS)] * 3
        + [shape(TOK, 2 * ROWS), shape(ROWS, KV)],
        in_specs=[SM, HBM, HBM, HBM],
        out_specs=[VM] * 11,
        scratch_shapes=[
            pltpu.VMEM((tiles, TILE, KV), F32),
            pltpu.SemaphoreType.DMA((14,)),
            pltpu.SemaphoreType.DMA((tiles,)),
        ],
        cost_estimate=cost(1),
        compiler_params=params(16),
        name="pack",
    )(place, acts, cot, master)
    return outs[:3], outs[3:6], outs[6:9], *outs[9:]


def group_sums(dtype, acts, cots, earlier=()):
    def kernel(*refs):
        a, c, out = refs[:4], refs[4:8], refs[-1]
        total = None
        for k in range(4):
            term = lax.dot_general(a[k][...], c[k][...], DIMS_T, preferred_element_type=F32)
            total = term if total is None else total + term
        out[...] = total.astype(dtype)

    def strip(first):
        return pl.BlockSpec((TOK, TILE), lambda j: (0, first // TILE + j))

    whole = pl.BlockSpec((TOK, KV), lambda j: (0, 0))
    return pl.pallas_call(
        kernel,
        out_shape=shape(HALF, KV, dtype=dtype),
        grid=(HALF // TILE,),
        in_specs=[strip(first) for _, first in acts] + [whole] * 4 + [ANY] * len(earlier),
        out_specs=pl.BlockSpec((TILE, KV), lambda j: (j, 0)),
        cost_estimate=cost(1),
        compiler_params=params(16),
        name="group_sums",
    )(*[a for a, _ in acts], *cots, *earlier)


def adam(half, core, own, received, master, first, second, earlier):
    tile = 64
    count = HALF // tile
    from_one = 0.5 / (1.0 - 0.9**STEP)
    from_two = 1.0 / math.sqrt(1.0 - 0.95**STEP)

    def kernel(core_ref, g_ref, got_ref, w_ref, m1_ref, m2_ref, *refs):
        upd_ref, keep, send, g, got, w, m1, m2, upd, sems, out_sems = refs[-11:]
        pairs = ((g_ref, g, 0), (got_ref, got, 0), (w_ref, w, 1), (m1_ref, m1, 1), (m2_ref, m2, 1))
        loads = []
        for t in range(count):
            loads.append(
                [
                    pltpu.make_async_copy(
                        src.at[pl.ds(t * tile + far * half * HALF, tile)], dst.at[t], sems.at[n, t]
                    )
                    for n, (src, dst, far) in enumerate(pairs)
                ]
            )
        for row in loads:
            for load in row:
                load.start()
        stores = []
        for t, row in enumerate(loads):
            for load in row:
                load.wait()
            grad = g[t] + got[t].astype(F32)
            one = 0.9 * m1[t] + 0.1 * grad
            two = 0.95 * m2[t] + 0.05 * grad * grad
            root = two * lax.rsqrt(two)
            new = w[t] - from_one * one / (root * from_two + 1e-8)
            upd[t] = new

            @pl.when(core_ref[0] == t % 2)
            def _():
                keep[t // 2] = new.astype(BF)

            @pl.when(core_ref[0] != t % 2)
            def _():
                send[t // 2] = new.astype(BF)

            store = pltpu.make_async_copy(
                upd.at[t], upd_ref.at[pl.ds(t * tile, tile)], out_sems.at[t]
            )
            store.start()
            stores.append(store)
        for store in stores:
            store.wait()

    return pl.pallas_call(
        kernel,
        out_shape=[shape(HALF, KV, dtype=F32), shape(4, 64, KV), shape(4, 64, KV)],
        in_specs=[SM, ANY, ANY, HBM, HBM, HBM] + [ANY] * len(earlier),
        out_specs=[ANY, VM, VM],
        scratch_shapes=[
            pltpu.VMEM((count, tile, KV), F32),
            pltpu.VMEM((count, tile, KV), BF),
        ]
        + [pltpu.VMEM((count, tile, KV), F32)] * 4
        + [pltpu.SemaphoreType.DMA((5, count)), pltpu.SemaphoreType.DMA((count,))],
        cost_estimate=cost(1),
        compiler_params=params(20),
        name="adam_step",
    )(core, own, received, master, first, second, *earlier)


def input_blocks(weight, weight_got, cots, earlier):
    count = ROWS // TILE

    def kernel(w0, w1, c0, c1, c2, c3, *refs):
        outs, joined = refs[-5:-1], refs[-1]
        step = pl.program_id(0)

        @pl.when(step == 0)
        def _():
            for k, c in enumerate((c0, c1, c2, c3)):
                joined[pl.ds(k * TOK, TOK), :] = c[...]

        def fill(w):
            product = lax.dot_general(joined[...], w[...], DIMS_N, preferred_element_type=F32)
            for k, out in enumerate(outs):
                out[...] = product[k * TOK : (k + 1) * TOK].astype(BF)

        @pl.when(step < count)
        def _():
            fill(w0)

        @pl.when(step >= count)
        def _():
            fill(w1)

    def tile(start):
        return pl.BlockSpec((TILE, KV), lambda j: (jnp.clip(j - start, 0, count - 1), 0))

    whole = pl.BlockSpec((TOK, KV), lambda j: (0, 0))
    return pl.pallas_call(
        kernel,
        out_shape=[pltpu.HBM((TOK, 2 * ROWS), BF)] * 4,
        grid=(2 * count,),
        in_specs=[tile(0), tile(count)] + [whole] * 4 + [ANY] * len(earlier),
        out_specs=[pl.BlockSpec((TOK, TILE), lambda j: (0, j))] * 4,
        scratch_shapes=[pltpu.VMEM((4 * TOK, KV), BF)],
        cost_estimate=cost(1),
        compiler_params=params(20),
        name="input_blocks",
    )(weight, weight_got, *cots, *earlier)


def assemble(place, blocks, earlier):
    def kernel(place_ref, *refs):
        ins, out, sems = refs[:4], refs[-2], refs[-1]
        zh, y = place_ref[0], place_ref[1]
        copies = []
        for k in range(4):
            for dz in range(2):
                block = lax.rem(zh + dz, 2) * 4 + lax.rem(y + 4 - k, 4)
                columns = pl.ds(pl.multiple_of(block * ROWS, ROWS), ROWS)
                part = ins[k].at[:, pl.ds(dz * ROWS, ROWS)]
                copies.append(
                    pltpu.make_async_copy(part, out.at[:, columns], sems.at[2 * k + dz])
                )
        for copy in copies:
            copy.start()
        for copy in copies:
            copy.wait()

    return pl.pallas_call(
        kernel,
        out_shape=shape(TOK, 8 * ROWS),
        in_specs=[SM] + [VM] * 4 + [ANY] * len(earlier),
        out_specs=ANY,
        scratch_shapes=[pltpu.SemaphoreType.DMA((8,))],
        cost_estimate=cost(1),
        compiler_params=params(8),
        name="assemble",
    )(place, *blocks, *earlier)


def core_sums(x_place, keep, received):
    def kernel(x_ref, keep_ref, got_ref, *outs):
        for dx in range(4):
            at = lax.rem(x_ref[0] + dx, 4)
            outs[dx][...] = (keep_ref[at].astype(F32) + got_ref[at].astype(F32)).astype(BF)

    return pl.pallas_call(
        kernel,
        out_shape=[shape(64, KV)] * 4,
        in_specs=[SM, VM, VM],
        out_specs=[VM] * 4,
        cost_estimate=cost(1),
        compiler_params=params(4),
        name="core_sums",
    )(x_place, keep, received)


def x_sums(half, zl, parts, anchor, momentum):
    def kernel(z_ref, p0, p1, p2, p3, w, m, wide, rounded):
        total = (p0[...].astype(F32) + p1[...].astype(F32)) + (
            p2[...].astype(F32) + p3[...].astype(F32)
        )
        wide[...] = total
        base = (16.0 / 1.33) * (-0.33 * w[...] - 0.567 * m[...])
        owner = jnp.broadcast_to(z_ref[0] == half, total.shape)
        rounded[...] = (total + jnp.where(owner, base, 0.0)).astype(BF)

    return pl.pallas_call(
        kernel,
        out_shape=[shape(64, KV, dtype=F32), shape(64, KV)],
        in_specs=[SM] + [VM] * 6,
        out_specs=[VM] * 2,
        cost_estimate=cost(1),
        compiler_params=params(4),
        name="x_sums",
    )(zl, *parts, anchor, momentum)


def outer_step(half, zl, mine, received, anchor, momentum, former):
    def kernel(z_ref, s, got, w, m, *refs):
        new_w, new_m, rounded = refs[-3:]
        total = s[...] + got[...].astype(F32)
        pseudo = w[...] - total / 16.0
        speed = 0.9 * m[...] + pseudo
        fresh = w[...] - 0.7 * (pseudo + 0.9 * speed)
        owner = jnp.broadcast_to(z_ref[0] == half, fresh.shape)
        rounded[...] = jnp.where(owner, fresh, (1.33 / 16.0) * total).astype(BF)
        if half:
            new_w[...] = jnp.where(owner, fresh, refs[0][...])
            new_m[...] = jnp.where(owner, speed, refs[1][...])
        else:
            new_w[...] = fresh
            new_m[...] = speed

    return pl.pallas_call(
        kernel,
        out_shape=[shape(64, KV, dtype=F32), shape(64, KV, dtype=F32), shape(64, KV)],
        in_specs=[SM] + [VM] * (4 + len(former)),
        out_specs=[VM] * 3,
        cost_estimate=cost(1),
        compiler_params=params(8),
        name="outer_step",
    )(zl, mine, received, anchor, momentum, *former)


def mix(half, place, updated, blocks, base):
    extra = [] if base is None else [base]

    def kernel(place_ref, upd, *refs):
        ins, out = refs[:8], refs[-1]
        dx = pl.program_id(0)
        for k in range(4):

            @pl.when(dx == k)
            def _():
                for dc in range(2):
                    core = lax.rem(place_ref[1] + dc, 2)
                    rows = pl.ds(pl.multiple_of(core * 64, 64), 64)
                    out[rows, :] = 0.5 * upd[rows, :] + 0.5 * ins[2 * k + dc][...].astype(F32)

    def here(dx, place):
        return (lax.rem(place[0] + 4 - dx, 4), 0)

    def there(dx, place):
        return (half * 4 + lax.rem(place[0] + 4 - dx, 4), 0)

    block = pl.BlockSpec((64, KV), lambda dx, place: (0, 0))
    return pl.pallas_call(
        kernel,
        out_shape=shape(ROWS, KV, dtype=F32),
        grid_spec=pltpu.PrefetchScalarGridSpec(
            num_scalar_prefetch=1,
            grid=(4,),
            in_specs=[pl.BlockSpec((128, KV), here)] + [block] * 8 + [ANY] * len(extra),
            out_specs=pl.BlockSpec((128, KV), there),
        ),
        input_output_aliases={10: 0} if extra else {},
        cost_estimate=cost(1),
        compiler_params=params(8),
        name="mix",
    )(place, updated, *blocks, *extra)


def shards(
    acts, cotangent, inner_weight, first_moment, second_moment, outer_weight, outer_momentum
):
    acts, cot, master = in_hbm(acts[0]), cotangent[0], in_hbm(inner_weight[0])
    moments = in_hbm(first_moment[0]), in_hbm(second_moment[0])
    anchor, momentum = outer_weight[0], outer_momentum[0]
    f, i = lax.axis_index("fsdp"), lax.axis_index("island")
    f_place = jnp.stack([f // 4, f % 4]).astype(jnp.int32)
    x_core = jnp.stack([(i // 2) % 4, i % 2]).astype(jnp.int32)
    zl, core = (i // 8).astype(jnp.int32)[None], (i % 2).astype(jnp.int32)[None]

    first, second, third, own, weight = pack(f_place, acts, in_hbm(cot), master)
    first = [along_y(a, k + 1) for k, a in enumerate(first)]
    weight_got = swap_z(weight)
    second = [along_y(gate(a, first[k]), k + 1) for k, a in enumerate(second)]
    third = [along_y(gate(a, second[k]), k + 1) for k, a in enumerate(third)]
    first = [in_hbm(a) for a in first]
    second = [in_hbm(a) for a in second]
    own = in_hbm(own)
    cots = [in_hbm(cot)] + first

    partial_0 = group_sums(BF, [(own, 0)] + [(a, KV) for a in first], cots)
    got_0 = swap_z(partial_0)
    partial_1 = group_sums(
        BF, [(own, HALF)] + [(a, 0) for a in second], cots, [weight_got]
    )
    got_1 = swap_z(partial_1)
    blocks = [in_hbm(b) for b in input_blocks(weight, weight_got, cots, [partial_1])]
    far = along_y(gate(blocks[2], *third), 2)

    mine = [(own, ROWS)] + [(a, 0) for a in third]
    mine = [(in_hbm(a), c) for a, c in mine]
    cots = [in_hbm(c) for c in cots]
    grad_0 = group_sums(F32, mine, cots, [blocks[0]])
    updated_0, keep_0, send_0 = adam(0, core, grad_0, got_0, master, *moments, [])

    def over_x(keep, send):
        sums = core_sums(x_core, keep, island_shift(send, 0, 0, 1))
        return [sums[0]] + [island_shift(sums[k], 0, k, 0) for k in (1, 2, 3)]

    def with_other_core(lines):
        return [part for line in lines for part in (line, island_shift(line, 0, 0, 1))]

    sums_0 = over_x(keep_0, send_0)
    grad_1 = group_sums(F32, [(a, c + HALF) for a, c in mine], cots)
    wide_0, rounded_0 = x_sums(0, zl, sums_0, anchor, momentum)
    updated_1, keep_1, send_1 = adam(
        1, core, grad_1, got_1, master, *moments, [rounded_0]
    )
    *former, fresh_0 = outer_step(
        0, zl, wide_0, island_shift(rounded_0, 1, 0, 0), anchor, momentum, []
    )
    sums_1 = over_x(keep_1, send_1)
    wide_1, rounded_1 = x_sums(1, zl, sums_1, anchor, momentum)
    near = [along_y(gate(blocks[4 - k], far, rounded_0), k) for k in (1, 3)]
    fresh_0 = gate(fresh_0, sums_1[1])
    lines_0 = with_other_core([fresh_0] + [island_shift(fresh_0, 0, k, 0) for k in (1, 2, 3)])
    *former, fresh_1 = outer_step(
        1, zl, wide_1, island_shift(rounded_1, 1, 0, 0), anchor, momentum, former
    )
    lines_1 = [island_shift(fresh_1, 0, k, 0) for k in (1, 2, 3)]
    mixed = mix(0, x_core, gate(updated_0, rounded_1), lines_0, None)
    input_grad = assemble(f_place, [blocks[0], near[0], far, near[1]], [fresh_1])
    lines_1[1] = gate(lines_1[1], in_hbm(input_grad))
    mixed = mix(1, x_core, updated_1, with_other_core([fresh_1] + lines_1), mixed)
    new_outer, new_momentum = former
    return (input_grad[None], mixed[None], new_outer[None], new_momentum[None])


def solution(mesh):
    by_island = P("island", "fsdp", None)
    by_rows = P("fsdp", "island", None)
    return jax.shard_map(
        shards,
        mesh=mesh,
        in_specs=(by_island,) * 5 + (by_rows,) * 2,
        out_specs=(by_island, by_island, by_rows, by_rows),
        check_vma=False,
    )
```
